256 devices in a mesh: pair: 8 (over z_lo, core), vocab: 32 (over x, y, z_hi).
Axes of the slice: x: 4, y: 4, z: 8 (z_hi: 2, z_lo: 4; z = z_hi * 4 + z_lo), core: 2. Of those that a mesh axis runs over, the one named last changes fastest.
Arguments:
- teacher_logits: bfloat16 [1024, 65536], P('pair', 'vocab'), may hold values from -20 to 260
- student_hidden: bfloat16 [1024, 4096], P('pair', 'vocab'), may hold values from -200 to 200
- head_weight: bfloat16 [4096, 65536], P('pair', 'vocab'), may hold values from -0.4 to 0.4
- head_bias: float32 [65536], P('vocab'), may hold values from -2.5 to 3.2
- pairing: int32 [8], replicated, may hold values from 0 to 7, as said below
- targets: int32 [1024], P('pair'), may hold values from 0 to 65535
Outputs:
- hidden_grad: bfloat16 [4096, 1024], P(('pair', 'vocab'))
- row_loss: float32 [1024], P('pair')
The draws below stay inside these ranges and needn't reach their ends.
Inputs may be any that keep to these rules, and one draw needn't show every extreme that they name: `pairing`: a permutation of the 8 groups.
All inputs are finite; a program needn't handle non-finite values.
Results may differ from the reference program's by a relative error of at most 0.0034.
Values may be sent and summed in bfloat16 or wider, within the bound.
No kernel may reach another device: no remote copies, remote signals or barrier semaphores. Data moves between devices by JAX's collectives and lax.ppermute only.
A program may use at most 128 MiB of HBM per device.

```python
import math
import jax
import jax.numpy as jnp
import numpy as np
from jax import lax

DS = 4096
ROWS = 128
V = 65536
TOKENS = 1024
N_PAIR = 8


def shared_weight(key):
    values = jnp.clip(jax.random.normal(key, (DS, V), jnp.float32), -6.0, 6.0)
    return values / math.sqrt(DS)


def draw_head_weight(key, part):
    weight = shared_weight(key)
    return weight.astype(jnp.bfloat16)


def draw_student_hidden(key, part):
    key = jax.random.fold_in(key, 2)
    first_key = jax.random.fold_in(key, 0)
    values = jnp.clip(3.0 * jax.random.normal(first_key, (TOKENS, DS), jnp.float32), -24.0, 24.0)
    return values.astype(jnp.bfloat16)


def plant_extremes(key, values):
    high_key, low_key = jax.random.split(key, 2)
    row_ids = jnp.arange(TOKENS)
    planted_rows = row_ids % 16 == 5
    high_col = jax.random.randint(high_key, (TOKENS,), 0, V)
    low_col = (high_col + 1 + jax.random.randint(low_key, (TOKENS,), 0, V - 1)) % V
    columns = jnp.arange(V)[None, :]
    is_high = planted_rows[:, None] & (columns == high_col[:, None])
    is_low = planted_rows[:, None] & (columns == low_col[:, None])
    values = jnp.where(is_high, 260.0, values)
    return jnp.where(is_low, -20.0, values)


def draw_teacher_logits(key, part):
    key = jax.random.fold_in(key, 3)
    plant_key = jax.random.fold_in(key, 11)
    columns = jnp.arange(V).astype(jnp.float32)
    column_bias = jnp.log1p(2.0 * columns / V)
    values = jnp.clip(3.0 * jax.random.normal(key, (TOKENS, V), jnp.float32), -18.0, 18.0) + column_bias[None, :]
    values = plant_extremes(plant_key, values)
    return values.astype(jnp.bfloat16)


def draw_head_bias(key, part):
    key = jax.random.fold_in(key, 4)
    columns = jnp.arange(V).astype(jnp.float32)
    column_bias = jnp.log1p(2.0 * columns / V)
    jitter = 0.5 * jnp.clip(jax.random.normal(key, (V,), jnp.float32), -4.0, 4.0)
    return column_bias + jitter


def draw_pairing(key, part):
    key = jax.random.fold_in(key, 5)
    scores = jax.random.randint(key, (N_PAIR,), 0, 1000000, dtype=jnp.int32) * N_PAIR + jnp.arange(N_PAIR, dtype=jnp.int32)
    return jnp.argsort(scores, stable=True).astype(jnp.int32)


def plant(entries, stream_key, least, largest):
    longest = entries.shape.index(max(entries.shape))
    spots = []
    for shift in (0, 1):
        where = [jax.random.randint(jax.random.fold_in(stream_key, axis), (), 0, length) for axis, length in enumerate(entries.shape)]
        where[longest] = (where[longest] + shift) % entries.shape[longest]
        spots.append(tuple(where))
    return entries.at[spots[0]].set(least).at[spots[1]].set(largest)


def cumulative_ranks(number_of, slope):
    loads = [(1 << 20) // math.isqrt(grade ** slope) + 1 for grade in range(1, number_of + 1)]
    scale = 1 + sum(loads) // (1 << 30)
    return np.cumsum(np.array([max(1, weight // scale) for weight in loads]))


def ranked_ids(stream_key, extent, count, lean):
    listing = cumulative_ranks(count, lean)
    ticket = jax.random.randint(jax.random.fold_in(stream_key, 1), extent, 0, int(listing[count - 1]))
    grade = jnp.searchsorted(jnp.asarray(listing, jnp.int32), ticket, side="right")
    return jax.random.permutation(jax.random.fold_in(stream_key, 2), count)[grade].astype(jnp.int32)


def setup_inputs(seed: int = 0) -> dict:
    arg_keys = jax.random.split(jax.random.key(seed), 7)
    teacher_logits = draw_teacher_logits(jax.random.fold_in(arg_keys[6], 71), 0)
    student_hidden = draw_student_hidden(jax.random.fold_in(arg_keys[6], 71), 0)
    head_weight = draw_head_weight(jax.random.fold_in(arg_keys[6], 71), 0)
    head_bias = draw_head_bias(jax.random.fold_in(arg_keys[6], 71), 0)
    pairing = draw_pairing(jax.random.fold_in(arg_keys[6], 71), 0)
    targets = plant(ranked_ids(arg_keys[5], (TOKENS,), V, 2), jax.random.fold_in(arg_keys[5], 3), 0, V - 1).astype(jnp.int32)
    return dict(teacher_logits=teacher_logits, student_hidden=student_hidden, head_weight=head_weight, head_bias=head_bias, pairing=pairing, targets=targets)


def reference(teacher_logits, student_hidden, head_weight, head_bias, pairing, targets):
    teacher = teacher_logits.astype(jnp.float32)
    teacher_lse = jax.nn.logsumexp(teacher, axis=1)
    log_teacher = teacher - teacher_lse[:, None]
    groups = jnp.arange(N_PAIR, dtype=jnp.int32)
    source = jnp.sum(groups[None, :] * (pairing[None, :] == groups[:, None]).astype(jnp.int32), axis=1)
    log_target = jnp.take(log_teacher.reshape(N_PAIR, ROWS, V), source, axis=0).reshape(TOKENS, V)
    target_prob = jnp.exp(log_target)
    logits = jnp.dot(student_hidden, head_weight, preferred_element_type=jnp.float32) + head_bias[None, :]
    student_lse = jax.nn.logsumexp(logits, axis=1)
    log_student = logits - student_lse[:, None]
    student_prob = jnp.exp(log_student)
    onehot = targets[:, None] == jnp.arange(V, dtype=jnp.int32)[None, :]
    row_loss = jnp.sum(target_prob * (log_target - log_student), axis=1) + student_lse - jnp.sum(jnp.where(onehot, logits, 0.0), axis=1)
    grad_logits = (2.0 * student_prob - target_prob - onehot.astype(jnp.float32)).astype(jnp.bfloat16)
    hidden_grad = lax.dot_general(head_weight, grad_logits, (((1,), (1,)), ((), ())), preferred_element_type=jnp.float32)
    return hidden_grad.astype(jnp.bfloat16), row_loss
```

```python
import jax
import jax.numpy as jnp
from jax import lax
from jax.experimental import pallas as pl
from jax.experimental.pallas import tpu as pltpu
from jax.sharding import Mesh, PartitionSpec as P

AXES = {"zl": 4, "co": 2, "x": 4, "y": 4, "zh": 2}
VMEM_BYTES = 56 * 1024 * 1024
F32 = jnp.float32
BF16 = jnp.bfloat16


def swap(value, axis, flip):
    return lax.ppermute(value, axis, [(i, i ^ flip) for i in range(AXES[axis])])


def swaps(value, axis):
    return [value] + [swap(value, axis, j) for j in range(1, AXES[axis])]


def add_all(parts):
    if len(parts) == 2:
        return parts[0] + parts[1]
    return (parts[0] + parts[1]) + (parts[2] + parts[3])


def in_order(parts, place):
    low = (place & 1) == 1
    if len(parts) == 2:
        return [jnp.where(low, parts[1], parts[0]), jnp.where(low, parts[0], parts[1])]
    high = (place & 2) == 2
    out = []
    for i in range(4):
        out.append(
            jnp.where(
                high,
                jnp.where(low, parts[i ^ 3], parts[i ^ 2]),
                jnp.where(low, parts[i ^ 1], parts[i]),
            )
        )
    return out


def join_stats(parts):
    peak = parts[0][:2]
    for part in parts[1:]:
        peak = jnp.maximum(peak, part[:2])
    total = add_all([part[2:] * jnp.exp(part[:2] - peak) for part in parts])
    return jnp.concatenate([peak, total], axis=0)


def logits_kernel(pos, *refs):
    own, other = refs[0:4], refs[4:8]
    first, second = refs[8:12], refs[12:16]
    bias, teacher_stat, logits, stat, x_buf, w_buf, sems = refs[16:]
    x, y, z, core = pos[0], pos[1], pos[2], pos[3]
    depth = own[0].shape[0]
    half, block = first[0].shape[1:]
    copies = []

    def copy(src, dst):
        made = pltpu.make_async_copy(src, dst, sems.at[len(copies)])
        made.start()
        copies.append(made)

    for j in range(4):
        for pieces, side in ((own, core), (other, 1 - core)):
            row = pl.multiple_of((2 * (z ^ j) + side) * depth, depth)
            copy(pieces[j], w_buf.at[pl.ds(row, depth), :])
    for j in range(4):
        for k in range(4):
            col = pl.multiple_of(((x ^ j) * 4 + (y ^ k)) * block, block)
            copy(first[j].at[k], x_buf.at[pl.ds(0, half), pl.ds(col, block)])
            copy(second[k].at[j], x_buf.at[pl.ds(half, half), pl.ds(col, block)])
    for made in copies:
        made.wait()
    cols = logits.shape[0]
    step = cols // 2
    for c in range(0, cols, step):
        part = jnp.dot(x_buf[...], w_buf[:, c : c + step], preferred_element_type=F32)
        part = part + bias[:, c : c + step]
        logits[c : c + step, :] = part.T
    values = logits[...]
    peak = jnp.max(values, axis=0, keepdims=True)
    stat[0:1, :] = peak
    stat[1:2, :] = teacher_stat[0:1, :]
    stat[2:3, :] = jnp.sum(jnp.exp(values - peak), axis=0, keepdims=True)
    stat[3:4, :] = teacher_stat[1:2, :]


def grad_kernel(pos, *refs):
    weights, pieces = refs[0:2], refs[2:6]
    first, second = refs[6:10], refs[10:14]
    w_buf, g_buf, sems = refs[14:]
    x, y, z = pos[0], pos[1], pos[2]
    quarter = pieces[0].shape[0]
    rows = weights[0].shape[0] // 16
    copies = []

    def copy(src, dst):
        made = pltpu.make_async_copy(src, dst, sems.at[len(copies)])
        made.start()
        copies.append(made)

    for j in range(4):
        row = pl.multiple_of((z ^ j) * quarter, quarter)
        copy(pieces[j], g_buf.at[pl.ds(row, quarter), :])
    for j in range(4):
        for k in range(4):
            row = pl.multiple_of(((x ^ j) * 4 + (y ^ k)) * rows, rows)
            for s in range(2):
                to = ((j * 4 + k) * 2 + s) * rows
                copy(weights[s].at[pl.ds(row, rows), :], w_buf.at[pl.ds(to, rows), :])
    for made in copies:
        made.wait()
    half = g_buf.shape[1] // 2
    group = 8 * rows
    for j in range(4):
        left = w_buf[j * group : (j + 1) * group, :]
        part = jnp.dot(left, g_buf[:, :half], preferred_element_type=F32)
        first[j][...] = part.reshape(first[j].shape)
        part = jnp.dot(left, g_buf[:, half:], preferred_element_type=F32)
        part = part.reshape(first[j].shape)
        for k in range(4):
            second[k][j] = part[k]


def call_logits(pos, own, other, first, second, bias, teacher_stat):
    depth, cols = own[0].shape
    half, block = first[0].shape[1:]
    rows, feats = 2 * half, 16 * block
    hbm = pl.BlockSpec(memory_space=pl.ANY)
    vmem = pl.BlockSpec(memory_space=pltpu.VMEM)
    return pl.pallas_call(
        logits_kernel,
        out_shape=(
            jax.ShapeDtypeStruct((cols, rows), F32),
            jax.ShapeDtypeStruct((4, rows), F32),
        ),
        in_specs=[pl.BlockSpec(memory_space=pltpu.SMEM)] + [hbm] * 16 + [vmem] * 2,
        out_specs=(vmem, vmem),
        scratch_shapes=[
            pltpu.VMEM((rows, feats), BF16),
            pltpu.VMEM((feats, cols), BF16),
            pltpu.SemaphoreType.DMA((40,)),
        ],
        compiler_params=pltpu.CompilerParams(vmem_limit_bytes=VMEM_BYTES),
        cost_estimate=pl.CostEstimate(
            flops=2 * rows * feats * cols,
            bytes_accessed=2 * feats * (rows + cols),
            transcendentals=rows * cols,
        ),
        name="logits_block",
    )(pos, *own, *other, *first, *second, bias, teacher_stat)


def call_grad(pos, weights, pieces):
    rows_in, cols = weights[0].shape
    quarter, tokens = pieces[0].shape
    rows = rows_in // 16
    hbm = pl.BlockSpec(memory_space=pl.ANY)
    vmem = pl.BlockSpec(memory_space=pltpu.VMEM)
    out = jax.ShapeDtypeStruct((4, 2 * rows, tokens // 2), F32)
    return pl.pallas_call(
        grad_kernel,
        out_shape=(out,) * 8,
        in_specs=[pl.BlockSpec(memory_space=pltpu.SMEM)] + [hbm] * 6,
        out_specs=(vmem,) * 8,
        scratch_shapes=[
            pltpu.VMEM((2 * rows_in, cols), BF16),
            pltpu.VMEM((cols, tokens), BF16),
            pltpu.SemaphoreType.DMA((36,)),
        ],
        compiler_params=pltpu.CompilerParams(vmem_limit_bytes=VMEM_BYTES),
        cost_estimate=pl.CostEstimate(
            flops=4 * rows_in * cols * tokens,
            bytes_accessed=4 * rows_in * cols + 2 * cols * tokens,
            transcendentals=0,
        ),
        name="grad_block",
    )(pos, *weights, *pieces)


def per_device(teacher_logits, student_hidden, head_weight, head_bias, pairing, targets):
    z, core, x, y, zh = [lax.axis_index(axis) for axis in AXES]
    pos = jnp.stack([x, y, z, core]).astype(jnp.int32)
    rows, vocab_cols = teacher_logits.shape
    quarter = vocab_cols // 4

    feats = in_order(swaps(student_hidden, "zh"), zh)
    feats = in_order(swaps(jnp.concatenate(feats, axis=1), "zl"), z)
    first = jnp.stack(swaps(jnp.concatenate(feats[:2], axis=0), "y"))
    second = jnp.stack(swaps(jnp.concatenate(feats[2:], axis=0), "x"))
    first, second = swaps(first, "x"), swaps(second, "y")

    own = []
    for j in range(4):
        part = lax.dynamic_slice_in_dim(head_weight, (z ^ j) * quarter, quarter, axis=1)
        own.append(swap(part, "zl", j) if j else part)
    other = [swap(part, "co", 1) for part in own]
    other_weight = swap(head_weight, "co", 1)

    flipped = teacher_logits.T
    teacher = []
    for j in range(4):
        part = lax.dynamic_slice_in_dim(flipped, (z ^ j) * quarter, quarter, axis=0)
        teacher.append(swap(part, "zl", j) if j else part)
    teacher = jnp.stack(teacher)
    teacher = jnp.concatenate([teacher, swap(teacher, "co", 1)], axis=0)
    picked = []
    for i in range(4):
        source = jnp.sum(jnp.arange(8, dtype=jnp.int32) * (pairing == 2 * i + core))
        place = ((source >> 1) ^ z) + 4 * ((source & 1) ^ core)
        picked.append(lax.dynamic_index_in_dim(teacher, place, axis=0, keepdims=False))
    teacher = jnp.concatenate(picked, axis=1).astype(F32)
    teacher_peak = jnp.max(teacher, axis=0, keepdims=True)
    teacher_sum = jnp.sum(jnp.exp(teacher - teacher_peak), axis=0, keepdims=True)
    teacher_stat = jnp.concatenate([teacher_peak, teacher_sum], axis=0)
    wanted = jnp.concatenate(in_order(swaps(targets, "zl"), z))

    bias = lax.dynamic_slice_in_dim(head_bias, z * quarter, quarter)[None, :]
    logits, stat = call_logits(pos, own, other, first, second, bias, teacher_stat)

    for axis in ("x", "y", "zl", "zh"):
        stat = join_stats(swaps(stat, axis))
    lse = stat[:2] + jnp.log(stat[2:])
    student_lse, teacher_lse = lse[0:1], lse[1:2]

    log_target = teacher - teacher_lse
    target_prob = jnp.exp(log_target)
    log_student = logits - student_lse
    base = (((x * 4 + y) * 2 + zh) * 4 + z) * quarter
    ids = base + lax.broadcasted_iota(jnp.int32, logits.shape, 0)
    onehot = ids == wanted[None, :]
    grad = 2.0 * jnp.exp(log_student) - target_prob - onehot.astype(F32)
    grad = grad.astype(BF16)
    loss = jnp.sum(
        target_prob * (log_target - log_student) - jnp.where(onehot, logits, 0.0), axis=0
    )
    alone = (x + y + z + zh) == 0
    loss = loss + jnp.where(alone, student_lse[0], 0.0)

    first = call_grad(pos, (head_weight, other_weight), swaps(grad, "zl"))
    first, second = first[:4], first[4:]
    for axis in ("zl", "x", "y", "zh"):
        loss = add_all(swaps(loss, axis))
    row_loss = lax.dynamic_slice_in_dim(loss, z * rows, rows)

    first = add_all([first[0]] + [swap(first[j], "x", j) for j in range(1, 4)])
    second = add_all([second[0]] + [swap(second[j], "y", j) for j in range(1, 4)])
    first = add_all([first[0]] + [swap(first[j], "y", j) for j in range(1, 4)])
    second = add_all([second[0]] + [swap(second[j], "x", j) for j in range(1, 4)])
    total = jnp.concatenate([first, second], axis=1)
    share = head_weight.shape[0] // 32
    total = total.reshape(2, 2, share, total.shape[1])
    mine = jnp.where(zh == 0, total[:, 0], total[:, 1])
    theirs = jnp.where(zh == 0, total[:, 1], total[:, 0])
    total = (mine + swap(theirs, "zh", 1)).astype(BF16)
    sides = in_order([total[0], swap(total[1], "co", 1)], core)
    sides = [side.reshape(share, 4, rows) for side in sides]
    hidden_grad = jnp.stack(sides, axis=2).reshape(share, 8 * rows)
    return hidden_grad, row_loss


def solution(mesh):
    fine = Mesh(mesh.devices.reshape(tuple(AXES.values())), tuple(AXES))
    pair, vocab = ("zl", "co"), ("x", "y", "zh")
    return jax.shard_map(
        per_device,
        mesh=fine,
        in_specs=(P(pair, vocab), P(pair, vocab), P(pair, vocab), P(vocab), P(), P(pair)),
        out_specs=(P(pair + vocab, None), P(pair)),
        check_vma=False,
    )
```

```python
import jax
import jax.numpy as jnp
from jax import lax
from jax.experimental import pallas as pl
from jax.experimental.pallas import tpu as pltpu
from jax.sharding import Mesh, PartitionSpec as P

AXES = {"zl": 4, "co": 2, "x": 4, "y": 4, "zh": 2}
VMEM_BYTES = 56 * 1024 * 1024
F32 = jnp.float32
BF16 = jnp.bfloat16


def swap(value, axis, flip):
    return lax.ppermute(value, axis, [(i, i ^ flip) for i in range(AXES[axis])])


def swaps(value, axis):
    return [value] + [swap(value, axis, j) for j in range(1, AXES[axis])]


def add_all(parts):
    if len(parts) == 2:
        return parts[0] + parts[1]
    return (parts[0] + parts[1]) + (parts[2] + parts[3])


def in_order(parts, place):
    low = (place & 1) == 1
    if len(parts) == 2:
        return [jnp.where(low, parts[1], parts[0]), jnp.where(low, parts[0], parts[1])]
    high = (place & 2) == 2
    out = []
    for i in range(4):
        out.append(
            jnp.where(
                high,
                jnp.where(low, parts[i ^ 3], parts[i ^ 2]),
                jnp.where(low, parts[i ^ 1], parts[i]),
            )
        )
    return out


def join_stats(parts):
    peak = parts[0][:2]
    for part in parts[1:]:
        peak = jnp.maximum(peak, part[:2])
    sums, divs = [], []
    for part in parts:
        scale = jnp.exp(part[:2] - peak)
        sums.append(part[2:4] * scale)
        divs.append(part[4:5] * scale[1:2])
    rest = add_all([part[5:] for part in parts])
    return jnp.concatenate([peak, add_all(sums), add_all(divs), rest], axis=0)


def logits_kernel(pairing, *refs):
    own, other = refs[0:4], refs[4:8]
    feats, bias, wanted, logits, teacher, stat, x_buf, w_buf, t_buf, sems = refs[8:]
    z, core, x, y, zh = [lax.axis_index(axis) for axis in AXES]
    rows = t_buf.shape[1]
    depth = own[0].shape[0] - rows
    block = feats.shape[2]
    copies = []

    def copy(src, dst):
        made = pltpu.make_async_copy(src, dst, sems.at[len(copies)])
        made.start()
        copies.append(made)

    for j in range(4):
        for pieces, side, place in ((own, core, j), (other, 1 - core, 4 + j)):
            row = pl.multiple_of((2 * (z ^ j) + side) * depth, depth)
            copy(pieces[j].at[pl.ds(0, depth), :], w_buf.at[pl.ds(row, depth), :])
            copy(pieces[j].at[pl.ds(depth, rows), :], t_buf.at[place])
    for j in range(16):
        copy(feats.at[j], x_buf.at[:, pl.ds(j * block, block)])
    for made in copies:
        made.wait()
    cols = logits.shape[0]
    base = (((x * 4 + y) * 2 + zh) * 4 + z) * cols
    step = cols // 2
    for c in range(0, cols, step):
        part = jnp.dot(x_buf[...], w_buf[:, c : c + step], preferred_element_type=F32)
        part = part + bias[:, pl.ds(pl.multiple_of(z * cols + c, step), step)]
        logits[c : c + step, :] = part.T
    values = logits[...]
    peak = jnp.max(values, axis=0, keepdims=True)
    for i in range(4):
        source = jnp.int32(0)
        for s in range(8):
            source = jnp.where(pairing[s] == 2 * i + core, s, source)
        place = ((source >> 1) ^ z) + 4 * ((source & 1) ^ core)
        teacher[:, i * rows : (i + 1) * rows] = t_buf[place].astype(F32).T
    target = teacher[...]
    target_peak = jnp.max(target, axis=0, keepdims=True)
    weight = jnp.exp(target - target_peak)
    ids = base + lax.broadcasted_iota(jnp.int32, values.shape, 0)
    hit = jnp.where(ids == wanted[...], values, 0.0)
    stat[...] = jnp.zeros_like(stat)
    stat[0:1, :] = peak
    stat[1:2, :] = target_peak
    stat[2:3, :] = jnp.sum(jnp.exp(values - peak), axis=0, keepdims=True)
    stat[3:4, :] = jnp.sum(weight, axis=0, keepdims=True)
    stat[4:5, :] = jnp.sum(weight * (target - values), axis=0, keepdims=True)
    stat[5:6, :] = jnp.sum(hit, axis=0, keepdims=True)


def grad_kernel(*refs):
    weights, pieces = refs[0:2], refs[2:6]
    first, second = refs[6:10], refs[10:14]
    w_buf, g_buf, sems = refs[14:]
    z, _, x, y, _ = [lax.axis_index(axis) for axis in AXES]
    quarter = pieces[0].shape[0]
    rows = weights[0].shape[0] // 16
    copies = []

    def copy(src, dst):
        made = pltpu.make_async_copy(src, dst, sems.at[len(copies)])
        made.start()
        copies.append(made)

    for j in range(4):
        row = pl.multiple_of((z ^ j) * quarter, quarter)
        copy(pieces[j], g_buf.at[pl.ds(row, quarter), :])
    for j in range(4):
        for k in range(4):
            row = pl.multiple_of(((x ^ j) * 4 + (y ^ k)) * rows, rows)
            for s in range(2):
                to = ((j * 4 + k) * 2 + s) * rows
                copy(weights[s].at[pl.ds(row, rows), :], w_buf.at[pl.ds(to, rows), :])
    for made in copies:
        made.wait()
    half = g_buf.shape[1] // 2
    group = 8 * rows
    for j in range(4):
        left = w_buf[j * group : (j + 1) * group, :]
        part = jnp.dot(left, g_buf[:, :half], preferred_element_type=F32)
        first[j][...] = part.reshape(first[j].shape)
        part = jnp.dot(left, g_buf[:, half:], preferred_element_type=F32)
        part = part.reshape(first[j].shape)
        for k in range(4):
            second[k][j] = part[k]


def call_logits(pairing, own, other, feats, bias, wanted):
    cols = own[0].shape[1]
    rows, depth = feats.shape[1], 16 * feats.shape[2]
    group = rows // 4
    hbm = pl.BlockSpec(memory_space=pl.ANY)
    vmem = pl.BlockSpec(memory_space=pltpu.VMEM)
    return pl.pallas_call(
        logits_kernel,
        out_shape=(
            jax.ShapeDtypeStruct((cols, rows), F32),
            jax.ShapeDtypeStruct((cols, rows), F32),
            jax.ShapeDtypeStruct((8, rows), F32),
        ),
        in_specs=[pl.BlockSpec(memory_space=pltpu.SMEM)] + [hbm] * 9 + [vmem] * 2,
        out_specs=(vmem, vmem, vmem),
        scratch_shapes=[
            pltpu.VMEM((rows, depth), BF16),
            pltpu.VMEM((depth, cols), BF16),
            pltpu.VMEM((8, group, cols), BF16),
            pltpu.SemaphoreType.DMA((32,)),
        ],
        compiler_params=pltpu.CompilerParams(vmem_limit_bytes=VMEM_BYTES),
        cost_estimate=pl.CostEstimate(
            flops=2 * rows * depth * cols,
            bytes_accessed=2 * depth * (rows + cols),
            transcendentals=rows * cols,
        ),
        name="logits_block",
    )(pairing, *own, *other, feats, bias, wanted)


def call_grad(weights, pieces):
    rows_in, cols = weights[0].shape
    quarter, tokens = pieces[0].shape
    rows = rows_in // 16
    hbm = pl.BlockSpec(memory_space=pl.ANY)
    vmem = pl.BlockSpec(memory_space=pltpu.VMEM)
    out = jax.ShapeDtypeStruct((4, 2 * rows, tokens // 2), F32)
    return pl.pallas_call(
        grad_kernel,
        out_shape=(out,) * 8,
        in_specs=[hbm] * 6,
        out_specs=(vmem,) * 8,
        scratch_shapes=[
            pltpu.VMEM((2 * rows_in, cols), BF16),
            pltpu.VMEM((cols, tokens), BF16),
            pltpu.SemaphoreType.DMA((36,)),
        ],
        compiler_params=pltpu.CompilerParams(vmem_limit_bytes=VMEM_BYTES),
        cost_estimate=pl.CostEstimate(
            flops=4 * rows_in * cols * tokens,
            bytes_accessed=4 * rows_in * cols + 2 * cols * tokens,
            transcendentals=0,
        ),
        name="grad_block",
    )(*weights, *pieces)


def after(value, *others):
    return lax.optimization_barrier((value, *others))[0]


def per_device(teacher_logits, student_hidden, head_weight, head_bias, pairing, targets):
    z, core, x, y, zh = [lax.axis_index(axis) for axis in AXES]
    rows, vocab_cols = teacher_logits.shape
    quarter = vocab_cols // 4
    base = (((x * 4 + y) * 2 + zh) * 4 + z) * quarter
    feats = in_order(swaps(student_hidden, "zh"), zh)
    gathered = swaps(jnp.concatenate(feats, axis=1), "zl")
    wanted = jnp.concatenate(in_order(swaps(after(targets, feats[0]), "zl"), z))[None, :]

    both = jnp.concatenate([head_weight, teacher_logits], axis=0)
    own = [lax.dynamic_slice_in_dim(both, (z ^ j) * quarter, quarter, axis=1) for j in range(4)]
    own[1:] = [swap(after(own[j], gathered[1]), "zl", j) for j in range(1, 4)]
    other = [swap(part, "co", 1) for part in own]

    feats = after(jnp.concatenate(in_order(gathered, z), axis=0), wanted)
    feats = lax.all_to_all(jnp.broadcast_to(feats, (16, *feats.shape)), ("x", "y"), 0, 0, tiled=True)
    logits, teacher, stat = call_logits(pairing, own, other, feats, head_bias[None, :], wanted)

    for axis, place in (("x", x), ("y", y), ("zl", z), ("zh", zh)):
        stat = join_stats(in_order(swaps(stat, axis), place))
    student_lse = stat[0:1] + jnp.log(stat[2:3])
    teacher_lse = stat[1:2] + jnp.log(stat[3:4])
    loss = stat[4:5] / stat[3:4] - teacher_lse + 2.0 * student_lse - stat[5:6]
    row_loss = lax.dynamic_slice_in_dim(loss[0], z * rows, rows)

    target_prob = jnp.exp(teacher - teacher_lse)
    ids = base + lax.broadcasted_iota(jnp.int32, logits.shape, 0)
    onehot = (ids == wanted).astype(F32)
    grad = (2.0 * jnp.exp(logits - student_lse) - target_prob - onehot).astype(BF16)

    other_weight = swap(after(head_weight, grad), "co", 1)
    first = call_grad((head_weight, other_weight), swaps(grad, "zl"))
    first, second = first[:4], first[4:]
    first = add_all([first[0]] + [swap(first[j], "x", j) for j in range(1, 4)])
    second = add_all([second[0]] + [swap(second[j], "y", j) for j in range(1, 4)])
    first = add_all([first[0]] + [swap(first[j], "y", j) for j in range(1, 4)])
    second = add_all([second[0]] + [swap(second[j], "x", j) for j in range(1, 4)])
    total = jnp.concatenate([first, second], axis=1)
    share = head_weight.shape[0] // 32
    total = total.reshape(2, 2, share, total.shape[1])
    mine = jnp.where(zh == 0, total[:, 0], total[:, 1])
    theirs = jnp.where(zh == 0, total[:, 1], total[:, 0])
    total = (mine + swap(theirs, "zh", 1)).astype(BF16)
    sides = in_order([total[0], swap(total[1], "co", 1)], core)
    sides = [side.reshape(share, 4, rows) for side in sides]
    hidden_grad = jnp.stack(sides, axis=2).reshape(share, 8 * rows)
    return hidden_grad, row_loss


def solution(mesh):
    fine = Mesh(mesh.devices.reshape(tuple(AXES.values())), tuple(AXES))
    pair, vocab = ("zl", "co"), ("x", "y", "zh")
    return jax.shard_map(
        per_device,
        mesh=fine,
        in_specs=(P(pair, vocab), P(pair, vocab), P(pair, vocab), P(vocab), P(), P(pair)),
        out_specs=(P(pair + vocab, None), P(pair)),
        check_vma=False,
    )
```

```python
import jax
import jax.numpy as jnp
from jax import lax
from jax.experimental import pallas as pl
from jax.experimental.pallas import tpu as pltpu
from jax.sharding import Mesh, PartitionSpec as P

AXES = {"zl": 4, "co": 2, "x": 4, "y": 4, "zh": 2}
VMEM_BYTES = 56 * 1024 * 1024
F32 = jnp.float32
BF16 = jnp.bfloat16


def swap(value, axis, flip):
    return lax.ppermute(value, axis, [(i, i ^ flip) for i in range(AXES[axis])])


def swaps(value, axis):
    return [value] + [swap(value, axis, j) for j in range(1, AXES[axis])]


def add_all(parts):
    if len(parts) == 2:
        return parts[0] + parts[1]
    return (parts[0] + parts[1]) + (parts[2] + parts[3])


def in_order(parts, place):
    low = (place & 1) == 1
    if len(parts) == 2:
        return [jnp.where(low, parts[1], parts[0]), jnp.where(low, parts[0], parts[1])]
    high = (place & 2) == 2
    out = []
    for i in range(4):
        out.append(
            jnp.where(
                high,
                jnp.where(low, parts[i ^ 3], parts[i ^ 2]),
                jnp.where(low, parts[i ^ 1], parts[i]),
            )
        )
    return out


def join_stats(parts):
    peak = parts[0][:2]
    for part in parts[1:]:
        peak = jnp.maximum(peak, part[:2])
    sums, divs = [], []
    for part in parts:
        scale = jnp.exp(part[:2] - peak)
        sums.append(part[2:4] * scale)
        divs.append(part[4:5] * scale[1:2])
    rest = add_all([part[5:] for part in parts])
    return jnp.concatenate([peak, add_all(sums), add_all(divs), rest], axis=0)


def logits_kernel(pairing, *refs):
    own, other = refs[0:4], refs[4:8]
    feats, bias, logits, teacher, wanted, stat, x_buf, w_buf, t_buf, d_buf, sems = refs[8:]
    z, core, x, y, zh = [lax.axis_index(axis) for axis in AXES]
    rows = t_buf.shape[1]
    depth = own[0].shape[0] - rows - 16
    block = feats.shape[2]
    cols = logits.shape[0]
    base = (((x * 4 + y) * 2 + zh) * 4 + z) * cols
    copies = []

    def copy(src, dst):
        made = pltpu.make_async_copy(src, dst, sems.at[len(copies)])
        made.start()
        copies.append(made)

    span = 4 * block
    for j in range(4):
        for pieces, side in ((own, core), (other, 1 - core)):
            row = pl.multiple_of((2 * (z ^ j) + side) * depth, depth)
            copy(pieces[j].at[pl.ds(0, depth), :], w_buf.at[pl.ds(row, depth), :])
        for k in range(4):
            col = pl.multiple_of((z ^ j) * span + k * block, block)
            copy(feats.at[(z ^ j) * 4 + k], x_buf.at[:, pl.ds(col, block)])
    for j in range(4):
        for pieces, place in ((own, j), (other, 4 + j)):
            copy(pieces[j].at[pl.ds(depth, rows), :], t_buf.at[place])
        copy(own[j].at[pl.ds(depth + rows, 16), :], d_buf.at[j])
    for j in range(4):
        for made in copies[6 * j : 6 * j + 6]:
            made.wait()
        at = pl.ds(pl.multiple_of((z ^ j) * span, span), span)
        part = jnp.dot(x_buf[:, at], w_buf[at, :], preferred_element_type=F32)
        if j == 0:
            teacher[...] = part + bias[:, pl.ds(pl.multiple_of(z * cols, cols), cols)]
        else:
            teacher[...] += part
    logits[...] = teacher[...].T
    for made in copies[24:]:
        made.wait()
    values = logits[...]
    peak = jnp.max(values, axis=0, keepdims=True)
    for j in range(4):
        digits = d_buf[j].astype(F32)
        ids = digits[0:1, :rows] * 256.0 + digits[1:2, :rows]
        at = pl.ds(pl.multiple_of((z ^ j) * rows, rows), rows)
        wanted[:, at] = ids.astype(jnp.int32)
    for i in range(4):
        source = jnp.int32(0)
        for s in range(8):
            source = jnp.where(pairing[s] == 2 * i + core, s, source)
        place = ((source >> 1) ^ z) + 4 * ((source & 1) ^ core)
        teacher[:, i * rows : (i + 1) * rows] = t_buf[place].astype(F32).T
    target = teacher[...]
    target_peak = jnp.max(target, axis=0, keepdims=True)
    weight = jnp.exp(target - target_peak)
    ids = base + lax.broadcasted_iota(jnp.int32, values.shape, 0)
    hit = jnp.where(ids == wanted[...], values, 0.0)
    stat[...] = jnp.zeros_like(stat)
    stat[0:1, :] = peak
    stat[1:2, :] = target_peak
    stat[2:3, :] = jnp.sum(jnp.exp(values - peak), axis=0, keepdims=True)
    stat[3:4, :] = jnp.sum(weight, axis=0, keepdims=True)
    stat[4:5, :] = jnp.sum(weight * (target - values), axis=0, keepdims=True)
    stat[5:6, :] = jnp.sum(hit, axis=0, keepdims=True)


def grad_kernel(*refs):
    weights, pieces = refs[0:2], refs[2:8]
    first, second = refs[8:12], refs[12:16]
    w_buf, g_buf, sems = refs[16:]
    z, _, x, y, _ = [lax.axis_index(axis) for axis in AXES]
    quarter = pieces[0].shape[0]
    rows = weights[0].shape[0] // 16
    copies = []

    def copy(src, dst):
        made = pltpu.make_async_copy(src, dst, sems.at[len(copies)])
        made.start()
        copies.append(made)

    for piece, j, part in zip(pieces, (0, 1, 2, 2, 3, 3), (0, 0, 0, 1, 0, 1)):
        size = piece.shape[0]
        row = pl.multiple_of((z ^ j) * quarter + part * size, size)
        copy(piece, g_buf.at[pl.ds(row, size), :])
    for j in range(4):
        for k in range(4):
            row = pl.multiple_of(((x ^ j) * 4 + (y ^ k)) * rows, rows)
            for s in range(2):
                to = ((j * 4 + k) * 2 + s) * rows
                copy(weights[s].at[pl.ds(row, rows), :], w_buf.at[pl.ds(to, rows), :])
    for made in copies[:6]:
        made.wait()
    half = g_buf.shape[1] // 2
    group = 8 * rows
    for j in range(4):
        for made in copies[6 + 8 * j : 14 + 8 * j]:
            made.wait()
        left = w_buf[j * group : (j + 1) * group, :]
        part = jnp.dot(left, g_buf[:, :half], preferred_element_type=F32)
        first[j][...] = part.reshape(first[j].shape)
        part = jnp.dot(left, g_buf[:, half:], preferred_element_type=F32)
        part = part.reshape(first[j].shape)
        for k in range(4):
            second[k][j] = part[k]


def call_logits(pairing, own, other, feats, bias):
    cols = own[0].shape[1]
    rows, depth = feats.shape[1], 16 * feats.shape[2]
    group = rows // 4
    hbm = pl.BlockSpec(memory_space=pl.ANY)
    vmem = pl.BlockSpec(memory_space=pltpu.VMEM)
    return pl.pallas_call(
        logits_kernel,
        out_shape=(
            jax.ShapeDtypeStruct((cols, rows), F32),
            jax.ShapeDtypeStruct((cols, rows), F32),
            jax.ShapeDtypeStruct((1, rows), jnp.int32),
            jax.ShapeDtypeStruct((8, rows), F32),
        ),
        in_specs=[pl.BlockSpec(memory_space=pltpu.SMEM)] + [hbm] * 9 + [vmem],
        out_specs=(vmem,) * 4,
        scratch_shapes=[
            pltpu.VMEM((rows, depth), BF16),
            pltpu.VMEM((depth, cols), BF16),
            pltpu.VMEM((8, group, cols), BF16),
            pltpu.VMEM((4, 16, cols), BF16),
            pltpu.SemaphoreType.DMA((36,)),
        ],
        compiler_params=pltpu.CompilerParams(vmem_limit_bytes=VMEM_BYTES),
        cost_estimate=pl.CostEstimate(
            flops=2 * rows * depth * cols,
            bytes_accessed=2 * depth * (rows + cols),
            transcendentals=rows * cols,
        ),
        name="logits_block",
    )(pairing, *own, *other, feats, bias)


def call_grad(weights, pieces):
    rows_in, cols = weights[0].shape
    quarter, tokens = pieces[0].shape
    rows = rows_in // 16
    hbm = pl.BlockSpec(memory_space=pl.ANY)
    vmem = pl.BlockSpec(memory_space=pltpu.VMEM)
    out = jax.ShapeDtypeStruct((4, 2 * rows, tokens // 2), F32)
    return pl.pallas_call(
        grad_kernel,
        out_shape=(out,) * 8,
        in_specs=[hbm] * 8,
        out_specs=(vmem,) * 8,
        scratch_shapes=[
            pltpu.VMEM((2 * rows_in, cols), BF16),
            pltpu.VMEM((cols, tokens), BF16),
            pltpu.SemaphoreType.DMA((38,)),
        ],
        compiler_params=pltpu.CompilerParams(vmem_limit_bytes=VMEM_BYTES),
        cost_estimate=pl.CostEstimate(
            flops=4 * rows_in * cols * tokens,
            bytes_accessed=4 * rows_in * cols + 2 * cols * tokens,
            transcendentals=0,
        ),
        name="grad_block",
    )(*weights, *pieces)


def after(value, *others):
    return lax.optimization_barrier((value, *others))[0]


def per_device(teacher_logits, student_hidden, head_weight, head_bias, pairing, targets):
    z, core, x, y, zh = [lax.axis_index(axis) for axis in AXES]
    rows, vocab_cols = teacher_logits.shape
    quarter = vocab_cols // 4
    base = (((x * 4 + y) * 2 + zh) * 4 + z) * quarter
    feats = in_order(swaps(student_hidden, "zh"), zh)
    gathered = swaps(jnp.concatenate(feats, axis=1), "zl")

    digits = jnp.stack([targets >> 8, targets & 255]).astype(BF16)
    digits = jnp.tile(jnp.pad(digits, ((0, 14), (0, quarter - rows))), (1, 4))
    both = jnp.concatenate([head_weight, teacher_logits, digits], axis=0)
    own = [lax.dynamic_slice_in_dim(both, (z ^ j) * quarter, quarter, axis=1) for j in range(4)]
    own[1:] = [swap(after(own[j], gathered[1]), "zl", j) for j in range(1, 4)]
    other = [swap(part, "co", 1) for part in own]

    feats = jnp.concatenate(in_order(gathered, z), axis=0)
    feats = lax.all_to_all(jnp.broadcast_to(feats, (16, *feats.shape)), ("x", "y"), 0, 0, tiled=True)
    logits, teacher, wanted, stat = call_logits(
        pairing, own, other, feats, head_bias[None, :]
    )

    for axis, place in (("x", x), ("y", y), ("zl", z), ("zh", zh)):
        stat = join_stats(in_order(swaps(stat, axis), place))
    student_lse = stat[0:1] + jnp.log(stat[2:3])
    teacher_lse = stat[1:2] + jnp.log(stat[3:4])
    loss = stat[4:5] / stat[3:4] - teacher_lse + 2.0 * student_lse - stat[5:6]
    row_loss = lax.dynamic_slice_in_dim(loss[0], z * rows, rows)

    target_prob = jnp.exp(teacher - teacher_lse)
    ids = base + lax.broadcasted_iota(jnp.int32, logits.shape, 0)
    onehot = (ids == wanted).astype(F32)
    grad = (2.0 * jnp.exp(logits - student_lse) - target_prob - onehot).astype(BF16)

    other_weight = swap(after(head_weight, grad), "co", 1)
    skips = [swap(part, "zl", 2) for part in jnp.split(grad, 2, axis=0)]
    pieces = [grad, swap(grad, "zl", 1), *skips, *[swap(part, "zl", 1) for part in skips]]
    first = call_grad((head_weight, other_weight), pieces)
    first, second = first[:4], first[4:]
    first = add_all([first[0]] + [swap(first[j], "x", j) for j in range(1, 4)])
    second = add_all([second[0]] + [swap(second[j], "y", j) for j in range(1, 4)])
    first = add_all([first[0]] + [swap(first[j], "y", j) for j in range(1, 4)])
    second = add_all([second[0]] + [swap(second[j], "x", j) for j in range(1, 4)])
    total = jnp.concatenate([first, second], axis=1)
    share = head_weight.shape[0] // 32
    total = total.reshape(2, 2, share, total.shape[1])
    mine = jnp.where(zh == 0, total[:, 0], total[:, 1])
    theirs = jnp.where(zh == 0, total[:, 1], total[:, 0])
    total = (mine + swap(theirs, "zh", 1)).astype(BF16)
    sides = in_order([total[0], swap(total[1], "co", 1)], core)
    sides = [side.reshape(share, 4, rows) for side in sides]
    hidden_grad = jnp.stack(sides, axis=2).reshape(share, 8 * rows)
    return hidden_grad, row_loss


def solution(mesh):
    fine = Mesh(mesh.devices.reshape(tuple(AXES.values())), tuple(AXES))
    pair, vocab = ("zl", "co"), ("x", "y", "zh")
    return jax.shard_map(
        per_device,
        mesh=fine,
        in_specs=(P(pair, vocab), P(pair, vocab), P(pair, vocab), P(vocab), P(), P(pair)),
        out_specs=(P(pair + vocab, None), P(pair)),
        check_vma=False,
    )
```

```python
import jax
import jax.numpy as jnp
from jax import lax
from jax.experimental import pallas as pl
from jax.experimental.pallas import tpu as pltpu
from jax.sharding import Mesh, PartitionSpec as P

AXES = {"zl": 4, "co": 2, "x": 4, "y": 4, "zh": 2}
VMEM_BYTES = 56 * 1024 * 1024
F32 = jnp.float32
BF16 = jnp.bfloat16


def swap(value, axis, flip):
    return lax.ppermute(value, axis, [(i, i ^ flip) for i in range(AXES[axis])])


def swaps(value, axis):
    return [value] + [swap(value, axis, j) for j in range(1, AXES[axis])]


def add_all(parts):
    if len(parts) == 2:
        return parts[0] + parts[1]
    return (parts[0] + parts[1]) + (parts[2] + parts[3])


def in_order(parts, place):
    low = (place & 1) == 1
    if len(parts) == 2:
        return [jnp.where(low, parts[1], parts[0]), jnp.where(low, parts[0], parts[1])]
    high = (place & 2) == 2
    out = []
    for i in range(4):
        out.append(
            jnp.where(
                high,
                jnp.where(low, parts[i ^ 3], parts[i ^ 2]),
                jnp.where(low, parts[i ^ 1], parts[i]),
            )
        )
    return out


def join_stats(parts):
    peak = parts[0][:2]
    for part in parts[1:]:
        peak = jnp.maximum(peak, part[:2])
    sums, divs = [], []
    for part in parts:
        scale = jnp.exp(part[:2] - peak)
        sums.append(part[2:4] * scale)
        divs.append(part[4:5] * scale[1:2])
    rest = add_all([part[5:] for part in parts])
    return jnp.concatenate([peak, add_all(sums), add_all(divs), rest], axis=0)


def logits_kernel(*refs):
    own, other = refs[0:4], refs[4:8]
    feats, bias, logits, stat, x_buf, w_buf, total, sems = refs[8:]
    z, core = lax.axis_index("zl"), lax.axis_index("co")
    depth = own[0].shape[0]
    block = feats.shape[2]
    cols = logits.shape[0]
    copies = []

    def copy(src, dst):
        made = pltpu.make_async_copy(src, dst, sems.at[len(copies)])
        made.start()
        copies.append(made)

    span = 4 * block
    for j in range(4):
        for pieces, side in ((own, core), (other, 1 - core)):
            row = pl.multiple_of((2 * (z ^ j) + side) * depth, depth)
            copy(pieces[j], w_buf.at[pl.ds(row, depth), :])
        for k in range(4):
            col = pl.multiple_of((z ^ j) * span + k * block, block)
            copy(feats.at[(z ^ j) * 4 + k], x_buf.at[:, pl.ds(col, block)])
    for j in range(4):
        for made in copies[6 * j : 6 * j + 6]:
            made.wait()
        at = pl.ds(pl.multiple_of((z ^ j) * span, span), span)
        part = jnp.dot(x_buf[:, at], w_buf[at, :], preferred_element_type=F32)
        if j == 0:
            total[...] = part + bias[:, pl.ds(pl.multiple_of(z * cols, cols), cols)]
        else:
            total[...] += part
    values = total[...].T
    logits[...] = values
    peak = jnp.max(values, axis=0, keepdims=True)
    stat[0:1, :] = peak
    stat[1:2, :] = jnp.sum(jnp.exp(values - peak), axis=0, keepdims=True)


def teacher_kernel(pairing, marks, logits, student, teacher, wanted, stat):
    z, core, x, y, zh = [lax.axis_index(axis) for axis in AXES]
    rows, cols = marks.shape[1] - 16, marks.shape[2]
    base = (((x * 4 + y) * 2 + zh) * 4 + z) * cols
    for j in range(4):
        digits = marks[j, rows:, :].astype(F32)
        ids = digits[0:1, :rows] * 256.0 + digits[1:2, :rows]
        at = pl.ds(pl.multiple_of((z ^ j) * rows, rows), rows)
        wanted[:, at] = ids.astype(jnp.int32)
    for i in range(4):
        source = jnp.int32(0)
        for s in range(8):
            source = jnp.where(pairing[s] == 2 * i + core, s, source)
        place = ((source >> 1) ^ z) + 4 * ((source & 1) ^ core)
        teacher[:, i * rows : (i + 1) * rows] = marks[place, :rows, :].astype(F32).T
    values = logits[...]
    target = teacher[...]
    target_peak = jnp.max(target, axis=0, keepdims=True)
    weight = jnp.exp(target - target_peak)
    ids = base + lax.broadcasted_iota(jnp.int32, values.shape, 0)
    hit = jnp.where(ids == wanted[...], values, 0.0)
    stat[...] = jnp.zeros_like(stat)
    stat[0:1, :] = student[0:1, :]
    stat[1:2, :] = target_peak
    stat[2:3, :] = student[1:2, :]
    stat[3:4, :] = jnp.sum(weight, axis=0, keepdims=True)
    stat[4:5, :] = jnp.sum(weight * (target - values), axis=0, keepdims=True)
    stat[5:6, :] = jnp.sum(hit, axis=0, keepdims=True)


def grad_kernel(*refs):
    weights, pieces = refs[0:2], refs[2:8]
    first, second = refs[8:12], refs[12:16]
    w_buf, g_buf, sems = refs[16:]
    z, _, x, y, _ = [lax.axis_index(axis) for axis in AXES]
    quarter = pieces[0].shape[0]
    rows = weights[0].shape[0] // 16
    copies = []

    def copy(src, dst):
        made = pltpu.make_async_copy(src, dst, sems.at[len(copies)])
        made.start()
        copies.append(made)

    for piece, j, part in zip(pieces, (0, 1, 2, 2, 3, 3), (0, 0, 0, 1, 0, 1)):
        size = piece.shape[0]
        row = pl.multiple_of((z ^ j) * quarter + part * size, size)
        copy(piece, g_buf.at[pl.ds(row, size), :])
    for j in range(4):
        for k in range(4):
            row = pl.multiple_of(((x ^ j) * 4 + (y ^ k)) * rows, rows)
            for s in range(2):
                to = ((j * 4 + k) * 2 + s) * rows
                copy(weights[s].at[pl.ds(row, rows), :], w_buf.at[pl.ds(to, rows), :])
    for made in copies[:6]:
        made.wait()
    half = g_buf.shape[1] // 2
    group = 8 * rows
    for j in range(4):
        for made in copies[6 + 8 * j : 14 + 8 * j]:
            made.wait()
        left = w_buf[j * group : (j + 1) * group, :]
        part = jnp.dot(left, g_buf[:, :half], preferred_element_type=F32)
        first[j][...] = part.reshape(first[j].shape)
        part = jnp.dot(left, g_buf[:, half:], preferred_element_type=F32)
        part = part.reshape(first[j].shape)
        for k in range(4):
            second[k][j] = part[k]


def call_logits(own, other, feats, bias):
    cols = own[0].shape[1]
    rows, depth = feats.shape[1], 16 * feats.shape[2]
    hbm = pl.BlockSpec(memory_space=pl.ANY)
    vmem = pl.BlockSpec(memory_space=pltpu.VMEM)
    return pl.pallas_call(
        logits_kernel,
        out_shape=(
            jax.ShapeDtypeStruct((cols, rows), F32),
            jax.ShapeDtypeStruct((2, rows), F32),
        ),
        in_specs=[hbm] * 9 + [vmem],
        out_specs=(vmem,) * 2,
        scratch_shapes=[
            pltpu.VMEM((rows, depth), BF16),
            pltpu.VMEM((depth, cols), BF16),
            pltpu.VMEM((rows, cols), F32),
            pltpu.SemaphoreType.DMA((24,)),
        ],
        compiler_params=pltpu.CompilerParams(vmem_limit_bytes=VMEM_BYTES),
        cost_estimate=pl.CostEstimate(
            flops=2 * rows * depth * cols,
            bytes_accessed=2 * depth * (rows + cols),
            transcendentals=rows * cols,
        ),
        name="logits_block",
    )(*own, *other, feats, bias)


def call_teacher(pairing, marks, logits, student):
    cols, rows = logits.shape
    vmem = pl.BlockSpec(memory_space=pltpu.VMEM)
    return pl.pallas_call(
        teacher_kernel,
        out_shape=(
            jax.ShapeDtypeStruct((cols, rows), F32),
            jax.ShapeDtypeStruct((1, rows), jnp.int32),
            jax.ShapeDtypeStruct((8, rows), F32),
        ),
        in_specs=[pl.BlockSpec(memory_space=pltpu.SMEM)] + [vmem] * 3,
        out_specs=(vmem,) * 3,
        compiler_params=pltpu.CompilerParams(vmem_limit_bytes=VMEM_BYTES),
        cost_estimate=pl.CostEstimate(
            flops=8 * rows * cols,
            bytes_accessed=12 * rows * cols,
            transcendentals=rows * cols,
        ),
        name="teacher_block",
    )(pairing, marks, logits, student)


def call_grad(weights, pieces):
    rows_in, cols = weights[0].shape
    quarter, tokens = pieces[0].shape
    rows = rows_in // 16
    hbm = pl.BlockSpec(memory_space=pl.ANY)
    vmem = pl.BlockSpec(memory_space=pltpu.VMEM)
    out = jax.ShapeDtypeStruct((4, 2 * rows, tokens // 2), F32)
    return pl.pallas_call(
        grad_kernel,
        out_shape=(out,) * 8,
        in_specs=[hbm] * 8,
        out_specs=(vmem,) * 8,
        scratch_shapes=[
            pltpu.VMEM((2 * rows_in, cols), BF16),
            pltpu.VMEM((cols, tokens), BF16),
            pltpu.SemaphoreType.DMA((38,)),
        ],
        compiler_params=pltpu.CompilerParams(vmem_limit_bytes=VMEM_BYTES),
        cost_estimate=pl.CostEstimate(
            flops=4 * rows_in * cols * tokens,
            bytes_accessed=4 * rows_in * cols + 2 * cols * tokens,
            transcendentals=0,
        ),
        name="grad_block",
    )(*weights, *pieces)


def after(value, *others):
    return lax.optimization_barrier((value, *others))[0]


def per_device(teacher_logits, student_hidden, head_weight, head_bias, pairing, targets):
    z, core, x, y, zh = [lax.axis_index(axis) for axis in AXES]
    rows, vocab_cols = teacher_logits.shape
    quarter = vocab_cols // 4
    base = (((x * 4 + y) * 2 + zh) * 4 + z) * quarter
    feats = in_order(swaps(student_hidden, "zh"), zh)
    gathered = swaps(jnp.concatenate(feats, axis=1), "zl")

    own = [
        lax.dynamic_slice_in_dim(head_weight, (z ^ j) * quarter, quarter, axis=1)
        for j in range(4)
    ]
    own[1:] = [swap(after(own[j], gathered[1]), "zl", j) for j in range(1, 4)]
    other = [swap(part, "co", 1) for part in own]

    digits = jnp.stack([targets >> 8, targets & 255]).astype(BF16)
    digits = jnp.tile(jnp.pad(digits, ((0, 14), (0, quarter - rows))), (1, 4))
    marks = jnp.concatenate([teacher_logits, digits], axis=0)
    marks = [lax.dynamic_slice_in_dim(marks, (z ^ j) * quarter, quarter, axis=1) for j in range(4)]
    marks[1:] = [swap(after(marks[j], *gathered[1:]), "zl", j) for j in range(1, 4)]
    feats = jnp.concatenate(in_order(gathered, z), axis=0)
    feats = lax.all_to_all(jnp.broadcast_to(feats, (16, *feats.shape)), ("x", "y"), 0, 0, tiled=True)
    logits, stat = call_logits(own, other, feats, head_bias[None, :])
    stat, *marks = lax.optimization_barrier((stat, *marks))
    marks = jnp.stack(marks)
    marks = jnp.concatenate([marks, swap(marks, "co", 1)], axis=0)
    teacher, wanted, stat = call_teacher(pairing, marks, logits, stat)

    for axis, place in (("x", x), ("y", y), ("zl", z), ("zh", zh)):
        stat = join_stats(in_order(swaps(stat, axis), place))
    student_lse = stat[0:1] + jnp.log(stat[2:3])
    teacher_lse = stat[1:2] + jnp.log(stat[3:4])
    loss = stat[4:5] / stat[3:4] - teacher_lse + 2.0 * student_lse - stat[5:6]
    row_loss = lax.dynamic_slice_in_dim(loss[0], z * rows, rows)

    target_prob = jnp.exp(teacher - teacher_lse)
    ids = base + lax.broadcasted_iota(jnp.int32, logits.shape, 0)
    onehot = (ids == wanted).astype(F32)
    grad = (2.0 * jnp.exp(logits - student_lse) - target_prob - onehot).astype(BF16)

    other_weight = swap(after(head_weight, own[1]), "co", 1)
    skips = [swap(part, "zl", 2) for part in jnp.split(grad, 2, axis=0)]
    pieces = [grad, swap(grad, "zl", 1), *skips, *[swap(part, "zl", 1) for part in skips]]
    first = call_grad((head_weight, other_weight), pieces)
    first, second = first[:4], first[4:]
    first = add_all([first[0]] + [swap(first[j], "x", j) for j in range(1, 4)])
    second = add_all([second[0]] + [swap(second[j], "y", j) for j in range(1, 4)])
    first = add_all([first[0]] + [swap(first[j], "y", j) for j in range(1, 4)])
    second = add_all([second[0]] + [swap(second[j], "x", j) for j in range(1, 4)])
    total = jnp.concatenate([first, second], axis=1)
    share = head_weight.shape[0] // 32
    total = total.reshape(2, 2, share, total.shape[1])
    mine = jnp.where(zh == 0, total[:, 0], total[:, 1])
    theirs = jnp.where(zh == 0, total[:, 1], total[:, 0])
    total = (mine + swap(theirs, "zh", 1)).astype(BF16)
    sides = in_order([total[0], swap(total[1], "co", 1)], core)
    sides = [side.reshape(share, 4, rows) for side in sides]
    hidden_grad = jnp.stack(sides, axis=2).reshape(share, 8 * rows)
    return hidden_grad, row_loss


def solution(mesh):
    fine = Mesh(mesh.devices.reshape(tuple(AXES.values())), tuple(AXES))
    pair, vocab = ("zl", "co"), ("x", "y", "zh")
    return jax.shard_map(
        per_device,
        mesh=fine,
        in_specs=(P(pair, vocab), P(pair, vocab), P(pair, vocab), P(vocab), P(), P(pair)),
        out_specs=(P(pair + vocab, None), P(pair)),
        check_vma=False,
    )
```

```python
import jax
import jax.numpy as jnp
from jax import lax
from jax.experimental import pallas as pl
from jax.experimental.pallas import tpu as pltpu
from jax.sharding import Mesh, PartitionSpec as P

AXES = {"zl": 4, "co": 2, "x": 4, "y": 4, "zh": 2}
VMEM_BYTES = 56 * 1024 * 1024
F32 = jnp.float32
BF16 = jnp.bfloat16


def swap(value, axis, flip):
    return lax.ppermute(value, axis, [(i, i ^ flip) for i in range(AXES[axis])])


def swaps(value, axis):
    return [value] + [swap(value, axis, j) for j in range(1, AXES[axis])]


def add_all(parts):
    if len(parts) == 2:
        return parts[0] + parts[1]
    return (parts[0] + parts[1]) + (parts[2] + parts[3])


def in_order(parts, place):
    low = (place & 1) == 1
    if len(parts) == 2:
        return [jnp.where(low, parts[1], parts[0]), jnp.where(low, parts[0], parts[1])]
    high = (place & 2) == 2
    out = []
    for i in range(4):
        out.append(
            jnp.where(
                high,
                jnp.where(low, parts[i ^ 3], parts[i ^ 2]),
                jnp.where(low, parts[i ^ 1], parts[i]),
            )
        )
    return out


def join_stats(parts):
    peak = parts[0][:2]
    for part in parts[1:]:
        peak = jnp.maximum(peak, part[:2])
    sums, divs = [], []
    for part in parts:
        scale = jnp.exp(part[:2] - peak)
        sums.append(part[2:4] * scale)
        divs.append(part[4:5] * scale[1:2])
    rest = add_all([part[5:] for part in parts])
    return jnp.concatenate([peak, add_all(sums), add_all(divs), rest], axis=0)


def logits_kernel(*refs):
    own, other = refs[0:4], refs[4:8]
    feats, bias, logits, stat, x_buf, w_buf, total, sems = refs[8:]
    z, core = lax.axis_index("zl"), lax.axis_index("co")
    depth = own[0].shape[0]
    block = feats.shape[2]
    cols = logits.shape[0]
    copies = []

    def copy(src, dst):
        made = pltpu.make_async_copy(src, dst, sems.at[len(copies)])
        made.start()
        copies.append(made)

    span = 4 * block
    for j in range(4):
        for pieces, side in ((own, core), (other, 1 - core)):
            row = pl.multiple_of((2 * (z ^ j) + side) * depth, depth)
            copy(pieces[j], w_buf.at[pl.ds(row, depth), :])
        for k in range(4):
            col = pl.multiple_of((z ^ j) * span + k * block, block)
            copy(feats.at[(z ^ j) * 4 + k], x_buf.at[:, pl.ds(col, block)])
    for j in range(4):
        for made in copies[6 * j : 6 * j + 6]:
            made.wait()
        at = pl.ds(pl.multiple_of((z ^ j) * span, span), span)
        part = jnp.dot(x_buf[:, at], w_buf[at, :], preferred_element_type=F32)
        if j == 0:
            total[...] = part + bias[:, pl.ds(pl.multiple_of(z * cols, cols), cols)]
        else:
            total[...] += part
    values = total[...].T
    logits[...] = values
    peak = jnp.max(values, axis=0, keepdims=True)
    stat[0:1, :] = peak
    stat[1:2, :] = jnp.sum(jnp.exp(values - peak), axis=0, keepdims=True)


def teacher_kernel(pairing, marks, logits, student, teacher, wanted, stat):
    z, core, x, y, zh = [lax.axis_index(axis) for axis in AXES]
    rows, cols = marks.shape[1] - 16, marks.shape[2]
    base = (((x * 4 + y) * 2 + zh) * 4 + z) * cols
    for j in range(4):
        digits = marks[j, rows:, :].astype(F32)
        ids = digits[0:1, :rows] * 256.0 + digits[1:2, :rows]
        at = pl.ds(pl.multiple_of((z ^ j) * rows, rows), rows)
        wanted[:, at] = ids.astype(jnp.int32)
    for i in range(4):
        source = jnp.int32(0)
        for s in range(8):
            source = jnp.where(pairing[s] == 2 * i + core, s, source)
        place = ((source >> 1) ^ z) + 4 * ((source & 1) ^ core)
        teacher[:, i * rows : (i + 1) * rows] = marks[place, :rows, :].astype(F32).T
    values = logits[...]
    target = teacher[...]
    target_peak = jnp.max(target, axis=0, keepdims=True)
    weight = jnp.exp(target - target_peak)
    ids = base + lax.broadcasted_iota(jnp.int32, values.shape, 0)
    hit = jnp.where(ids == wanted[...], values, 0.0)
    stat[...] = jnp.zeros_like(stat)
    stat[0:1, :] = student[0:1, :]
    stat[1:2, :] = target_peak
    stat[2:3, :] = student[1:2, :]
    stat[3:4, :] = jnp.sum(weight, axis=0, keepdims=True)
    stat[4:5, :] = jnp.sum(weight * (target - values), axis=0, keepdims=True)
    stat[5:6, :] = jnp.sum(hit, axis=0, keepdims=True)


def grad_kernel(*refs):
    weights, pieces = refs[0:2], refs[2:8]
    first, second = refs[8:12], refs[12:16]
    w_buf, g_buf, sems = refs[16:]
    z, _, x, y, _ = [lax.axis_index(axis) for axis in AXES]
    quarter = pieces[0].shape[0]
    rows = weights[0].shape[0] // 16
    copies = []

    def copy(src, dst):
        made = pltpu.make_async_copy(src, dst, sems.at[len(copies)])
        made.start()
        copies.append(made)

    for piece, j, part in zip(pieces, (0, 1, 2, 2, 3, 3), (0, 0, 0, 1, 0, 1)):
        size = piece.shape[0]
        row = pl.multiple_of((z ^ j) * quarter + part * size, size)
        copy(piece, g_buf.at[pl.ds(row, size), :])
    for j in range(4):
        for k in range(4):
            row = pl.multiple_of(((x ^ j) * 4 + (y ^ k)) * rows, rows)
            for s in range(2):
                to = ((j * 4 + k) * 2 + s) * rows
                copy(weights[s].at[pl.ds(row, rows), :], w_buf.at[pl.ds(to, rows), :])
    for made in copies[:6]:
        made.wait()
    half = g_buf.shape[1] // 2
    group = 8 * rows
    for j in range(4):
        for made in copies[6 + 8 * j : 14 + 8 * j]:
            made.wait()
        left = w_buf[j * group : (j + 1) * group, :]
        part = jnp.dot(left, g_buf[:, :half], preferred_element_type=F32)
        first[j][...] = part.reshape(first[j].shape)
        part = jnp.dot(left, g_buf[:, half:], preferred_element_type=F32)
        part = part.reshape(first[j].shape)
        for k in range(4):
            second[k][j] = part[k]


def call_logits(own, other, feats, bias):
    cols = own[0].shape[1]
    rows, depth = feats.shape[1], 16 * feats.shape[2]
    hbm = pl.BlockSpec(memory_space=pl.ANY)
    vmem = pl.BlockSpec(memory_space=pltpu.VMEM)
    return pl.pallas_call(
        logits_kernel,
        out_shape=(
            jax.ShapeDtypeStruct((cols, rows), F32),
            jax.ShapeDtypeStruct((2, rows), F32),
        ),
        in_specs=[hbm] * 9 + [vmem],
        out_specs=(vmem,) * 2,
        scratch_shapes=[
            pltpu.VMEM((rows, depth), BF16),
            pltpu.VMEM((depth, cols), BF16),
            pltpu.VMEM((rows, cols), F32),
            pltpu.SemaphoreType.DMA((24,)),
        ],
        compiler_params=pltpu.CompilerParams(vmem_limit_bytes=VMEM_BYTES),
        cost_estimate=pl.CostEstimate(
            flops=2 * rows * depth * cols,
            bytes_accessed=2 * depth * (rows + cols),
            transcendentals=rows * cols,
        ),
        name="logits_block",
    )(*own, *other, feats, bias)


def call_teacher(pairing, marks, logits, student):
    cols, rows = logits.shape
    vmem = pl.BlockSpec(memory_space=pltpu.VMEM)
    return pl.pallas_call(
        teacher_kernel,
        out_shape=(
            jax.ShapeDtypeStruct((cols, rows), F32),
            jax.ShapeDtypeStruct((1, rows), jnp.int32),
            jax.ShapeDtypeStruct((8, rows), F32),
        ),
        in_specs=[pl.BlockSpec(memory_space=pltpu.SMEM)] + [vmem] * 3,
        out_specs=(vmem,) * 3,
        compiler_params=pltpu.CompilerParams(vmem_limit_bytes=VMEM_BYTES // 4),
        cost_estimate=pl.CostEstimate(
            flops=8 * rows * cols,
            bytes_accessed=12 * rows * cols,
            transcendentals=rows * cols,
        ),
        name="teacher_block",
    )(pairing, marks, logits, student)


def call_grad(weights, pieces):
    rows_in, cols = weights[0].shape
    quarter, tokens = pieces[0].shape
    rows = rows_in // 16
    hbm = pl.BlockSpec(memory_space=pl.ANY)
    vmem = pl.BlockSpec(memory_space=pltpu.VMEM)
    out = jax.ShapeDtypeStruct((4, 2 * rows, tokens // 2), F32)
    return pl.pallas_call(
        grad_kernel,
        out_shape=(out,) * 8,
        in_specs=[hbm] * 8,
        out_specs=(vmem,) * 8,
        scratch_shapes=[
            pltpu.VMEM((2 * rows_in, cols), BF16),
            pltpu.VMEM((cols, tokens), BF16),
            pltpu.SemaphoreType.DMA((38,)),
        ],
        compiler_params=pltpu.CompilerParams(vmem_limit_bytes=VMEM_BYTES),
        cost_estimate=pl.CostEstimate(
            flops=4 * rows_in * cols * tokens,
            bytes_accessed=4 * rows_in * cols + 2 * cols * tokens,
            transcendentals=0,
        ),
        name="grad_block",
    )(*weights, *pieces)


def after(value, *others):
    return lax.optimization_barrier((value, *others))[0]


def per_device(teacher_logits, student_hidden, head_weight, head_bias, pairing, targets):
    z, core, x, y, zh = [lax.axis_index(axis) for axis in AXES]
    rows, vocab_cols = teacher_logits.shape
    quarter = vocab_cols // 4
    base = (((x * 4 + y) * 2 + zh) * 4 + z) * quarter
    feats = in_order(swaps(student_hidden, "zh"), zh)
    gathered = swaps(jnp.concatenate(feats, axis=1), "zl")

    own = [
        lax.dynamic_slice_in_dim(head_weight, (z ^ j) * quarter, quarter, axis=1)
        for j in range(4)
    ]
    own[1:] = [swap(after(own[j], gathered[1]), "zl", j) for j in range(1, 4)]
    other = [swap(part, "co", 1) for part in own]

    digits = jnp.stack([targets >> 8, targets & 255]).astype(BF16)
    digits = jnp.tile(jnp.pad(digits, ((0, 14), (0, quarter - rows))), (1, 4))
    marks = jnp.concatenate([teacher_logits, digits], axis=0)
    marks = [lax.dynamic_slice_in_dim(marks, (z ^ j) * quarter, quarter, axis=1) for j in range(4)]
    marks[1:] = [swap(after(marks[j], *gathered[1:]), "zl", j) for j in range(1, 4)]
    feats = jnp.concatenate(in_order(gathered, z), axis=0)
    feats = lax.all_to_all(jnp.broadcast_to(feats, (16, *feats.shape)), ("x", "y"), 0, 0, tiled=True)
    logits, stat = call_logits(own, other, feats, head_bias[None, :])
    stat, *marks = lax.optimization_barrier((stat, *marks))
    marks = jnp.stack(marks)
    marks = jnp.concatenate([marks, swap(marks, "co", 1)], axis=0)
    teacher, wanted, stat = call_teacher(pairing, marks, logits, stat)

    for axis, place in (("x", x), ("y", y), ("zl", z), ("zh", zh)):
        stat = join_stats(in_order(swaps(stat, axis), place))
    student_lse = stat[0:1] + jnp.log(stat[2:3])
    teacher_lse = stat[1:2] + jnp.log(stat[3:4])
    loss = stat[4:5] / stat[3:4] - teacher_lse + 2.0 * student_lse - stat[5:6]
    row_loss = lax.dynamic_slice_in_dim(loss[0], z * rows, rows)

    target_prob = jnp.exp(teacher - teacher_lse)
    ids = base + lax.broadcasted_iota(jnp.int32, logits.shape, 0)
    onehot = (ids == wanted).astype(F32)
    grad = (2.0 * jnp.exp(logits - student_lse) - target_prob - onehot).astype(BF16)

    other_weight = swap(after(head_weight, own[1]), "co", 1)
    skips = [swap(part, "zl", 2) for part in jnp.split(grad, 2, axis=0)]
    pieces = [grad, swap(grad, "zl", 1), *skips, *[swap(part, "zl", 1) for part in skips]]
    first = call_grad((head_weight, other_weight), pieces)
    first, second = first[:4], first[4:]
    first = add_all([first[0]] + [swap(first[j], "x", j) for j in range(1, 4)])
    second = add_all([second[0]] + [swap(second[j], "y", j) for j in range(1, 4)])
    first = add_all([first[0]] + [swap(first[j], "y", j) for j in range(1, 4)])
    second = add_all([second[0]] + [swap(second[j], "x", j) for j in range(1, 4)])
    total = jnp.concatenate([first, second], axis=1)
    share = head_weight.shape[0] // 32
    total = total.reshape(2, 2, share, total.shape[1])
    mine = jnp.where(zh == 0, total[:, 0], total[:, 1])
    theirs = jnp.where(zh == 0, total[:, 1], total[:, 0])
    total = (mine + swap(theirs, "zh", 1)).astype(BF16)
    sides = in_order([total[0], swap(total[1], "co", 1)], core)
    sides = [side.reshape(share, 4, rows) for side in sides]
    hidden_grad = jnp.stack(sides, axis=2).reshape(share, 8 * rows)
    return hidden_grad, row_loss


def solution(mesh):
    fine = Mesh(mesh.devices.reshape(tuple(AXES.values())), tuple(AXES))
    pair, vocab = ("zl", "co"), ("x", "y", "zh")
    return jax.shard_map(
        per_device,
        mesh=fine,
        in_specs=(P(pair, vocab), P(pair, vocab), P(pair, vocab), P(vocab), P(), P(pair)),
        out_specs=(P(pair + vocab, None), P(pair)),
        check_vma=False,
    )
```
